32 devices in a mesh: region: 2 (over core), space: 16 (over z, y, x).
Axes of the slice: x: 2, y: 2, z: 4, core: 2. Of those that a mesh axis runs over, the one named last changes fastest.
Arguments:
- f_cells: float32 [2, 128, 128, 128], P('region', 'space'), may hold values from -6 to 6
- g_mortar: float32 [2, 4096], P('region', 'space'), may hold values from -6 to 6
- mask_cells: int32 [2, 128, 128, 128], P('region', 'space'), may hold values 0 or 1
- zone_ids: int32 [2, 128, 128, 128], P('region', 'space'), may hold values from 0 to 15
- zone_coef: float32 [16], replicated, may hold values from 0.02 to 2
- mort_index: int32 [16, 2048], P('space'), may hold values from 0 to 511
- face_stokes: int32 [16, 2048], P('space'), may hold values from 0 to 1023
- face_darcy: int32 [16, 2048], P('space'), may hold values from 0 to 1023
- mort_weight: float32 [16, 2048], P('space'), may hold values from 0.25 to 1
- tile_count: int32 [16, 16], P('space'), may hold values from 1 to 128, as said below
Outputs:
- solution_cells: float32 [2, 128, 128, 128], P('region', 'space')
- solution_mortar: float32 [2, 4096], P('region', 'space')
The draws below stay inside these ranges and needn't reach their ends.
Inputs may be any that keep to these rules, and one draw needn't show every extreme that they name: `tile_count`: in every slab pair some tile has all 128 rows valid.
All inputs are finite; a program needn't handle non-finite values. No bound on the sum of `mask_cells` on one device may be relied on, other than what follows from the above.
Results may differ from the reference program's by a relative error of at most 0.00011.
Values sent between devices are 32-bit elements; how exact they have to be, the bound alone decides.
A program may use at most 64 MiB of HBM per device.

```python
import math
import jax
import jax.numpy as jnp

CY = 128
CZ = 128
ZONES = 16
ITERS = 4
NX = 128
FACE = 1024
MORT = 256
TILES = 16
LIST = 2048
N_SPACE = 16


def draw_tile_count(key, part):
    key = jax.random.fold_in(key, 7)
    first_key, second_key = jax.random.split(key)
    counts = jax.random.randint(first_key, (N_SPACE, TILES), 1, 129)
    chosen = jax.random.randint(second_key, (N_SPACE, 1), 0, TILES)
    return jnp.where(jnp.arange(TILES)[None, :] == chosen, 128, counts).astype(jnp.int32)


def touch_ends(array, key, low, high):
    longest = array.shape.index(max(array.shape))
    spots = []
    for shift in (0, 1):
        where = [jax.random.randint(jax.random.fold_in(key, axis), (), 0, length) for axis, length in enumerate(array.shape)]
        where[longest] = (where[longest] + shift) % array.shape[longest]
        spots.append(tuple(where))
    return array.at[spots[0]].set(low).at[spots[1]].set(high)


def shard_levels(rng, extent, cuts, low, largest):
    loudness, own = 1.0, jax.random.fold_in(rng, 6)
    for dim, blocks in cuts:
        draws = jnp.exp(jax.random.uniform(jax.random.fold_in(own, dim), (blocks,), jnp.float32, low / len(cuts), largest / len(cuts)))
        loudness = loudness * jnp.repeat(draws, extent[dim] // blocks).reshape([-1 if axis == dim else 1 for axis in range(len(extent))])
    return loudness


def normal_values(own_key, dims, width, bound, cuts=(), kind=jnp.bfloat16):
    loudness = shard_levels(own_key, dims, cuts, -0.22, 0.18) if cuts else 1.0
    values = jax.random.normal(own_key, dims, jnp.float32) * width * loudness
    return jnp.minimum(jnp.maximum(values, -bound), bound).astype(kind)


def setup_inputs(seed: int = 0) -> dict:
    key_of = jax.random.split(jax.random.key(seed), 11)
    return {
        "f_cells": normal_values(key_of[0], (2, NX, CY, CZ), 1.0, 6.0, ((0, 2), (1, 16)), jnp.float32),
        "g_mortar": normal_values(key_of[1], (2, N_SPACE * MORT), 1.0, 6.0, ((0, 2), (1, 16)), jnp.float32),
        "mask_cells": touch_ends((jax.random.randint(key_of[2], (2, NX, CY, CZ), 0, 10) < 9).astype(jnp.int32), jax.random.fold_in(key_of[2], 1), 0, 1),
        "zone_ids": touch_ends(jax.random.randint(key_of[3], (2, NX, CY, CZ), 0, ZONES), jax.random.fold_in(key_of[3], 1), 0, ZONES - 1).astype(jnp.int32),
        "zone_coef": jnp.clip(jnp.exp(jax.random.uniform(key_of[4], (ZONES,), jnp.float32, math.log(0.02), math.log(2.0))), 0.02, 2.0),
        "mort_index": touch_ends(jax.random.randint(key_of[5], (N_SPACE, LIST), 0, 2 * MORT), jax.random.fold_in(key_of[5], 1), 0, (2 * MORT) - 1).astype(jnp.int32),
        "face_stokes": touch_ends(jax.random.randint(key_of[6], (N_SPACE, LIST), 0, FACE), jax.random.fold_in(key_of[6], 1), 0, FACE - 1).astype(jnp.int32),
        "face_darcy": touch_ends(jax.random.randint(key_of[7], (N_SPACE, LIST), 0, FACE), jax.random.fold_in(key_of[7], 1), 0, FACE - 1).astype(jnp.int32),
        "mort_weight": jnp.clip(0.25 + 0.75 * jax.random.uniform(key_of[8], (N_SPACE, LIST), jnp.float32) ** shard_levels(key_of[8], (N_SPACE, LIST), ((0, 16),), -0.2, 0.2), 0.25, 1.0),
        "tile_count": draw_tile_count(jax.random.fold_in(key_of[10], 71), 0),
    }


OMEGA = 0.8
STAB = 0.05

def stencil_sum(values):
    padded = jnp.pad(values, ((0, 0), (1, 1), (1, 1), (1, 1)))
    total = padded[:, 2:, 1:-1, 1:-1] + padded[:, :-2, 1:-1, 1:-1]
    total = total + padded[:, 1:-1, 2:, 1:-1] + padded[:, 1:-1, :-2, 1:-1]
    return total + padded[:, 1:-1, 1:-1, 2:] + padded[:, 1:-1, 1:-1, :-2]

def fine_apply(cells, active, react):
    return active * ((6.0 + react) * cells - stencil_sum(active * cells)) + (1.0 - active) * cells

def coarsen(values):
    values = values[:, 0::2] + values[:, 1::2]
    values = values[:, :, 0::2] + values[:, :, 1::2]
    return values[:, :, :, 0::2] + values[:, :, :, 1::2]

def refine(values):
    return jnp.repeat(jnp.repeat(jnp.repeat(values, 2, axis=1), 2, axis=2), 2, axis=3)

def vcycle(resid, active, react, fine_diag, coarse_diag):
    first = OMEGA * resid / fine_diag
    coarse_rhs = coarsen(resid - fine_apply(first, active, react))
    sweep = OMEGA * coarse_rhs / coarse_diag
    coarse_res = coarse_rhs - (coarse_diag * sweep - 2.0 * stencil_sum(sweep))
    sweep = sweep + OMEGA * coarse_res / coarse_diag
    second = first + refine(sweep)
    return second + OMEGA * (resid - fine_apply(second, active, react)) / fine_diag

def pair_view(mults):
    return jnp.concatenate([mults[0].reshape(N_SPACE, MORT), mults[1].reshape(N_SPACE, MORT)], axis=1)

def unpair(paired):
    return jnp.stack([paired[:, :MORT].reshape(-1), paired[:, MORT:].reshape(-1)])

def coupling_rows(free_face, porous_face, mort_list, stokes_list, darcy_list, margin_coef):
    term = margin_coef * (free_face[stokes_list] - porous_face[darcy_list])
    return jax.ops.segment_sum(term, mort_list, num_segments=2 * MORT)

def coupling_cols(paired, mort_list, stokes_list, darcy_list, margin_coef):
    values = margin_coef * paired[mort_list]
    free_add = jax.ops.segment_sum(values, stokes_list, num_segments=FACE)
    porous_add = -jax.ops.segment_sum(values, darcy_list, num_segments=FACE)
    return (free_add, porous_add)

def combine(first, second, scale_one, scale_two):
    return (scale_one * first[0] + scale_two * second[0], scale_one * first[1] + scale_two * second[1])

def rotation(alpha_now, beta_now, cosine, sine_val, delta_bar, epsilon, phi_bar):
    old_eps = epsilon
    delta_val = cosine * delta_bar + sine_val * alpha_now
    gamma_bar = sine_val * delta_bar - cosine * alpha_now
    epsilon = sine_val * beta_now
    delta_bar = -cosine * beta_now
    gamma_val = jnp.sqrt(gamma_bar * gamma_bar + beta_now * beta_now)
    cosine = gamma_bar / gamma_val
    sine_val = beta_now / gamma_val
    phi_step = cosine * phi_bar
    phi_bar = sine_val * phi_bar
    return (old_eps, delta_val, gamma_val, phi_step, cosine, sine_val, delta_bar, epsilon, phi_bar)

def reference(f_cells, g_mortar, mask_cells, zone_ids, zone_coef, mort_index, face_stokes, face_darcy, mort_weight, tile_count):
    active = mask_cells.astype(jnp.float32)
    react = zone_coef[zone_ids]
    fine_diag = active * (6.0 + react) + (1.0 - active)
    coarse_diag = 2.0 * (6.0 + 0.125 * coarsen(active * react))
    rows_iota = jnp.arange(LIST, dtype=jnp.int32)
    valid = (rows_iota % 128)[None, :] < jnp.repeat(tile_count, 128, axis=1)
    margin_coef = jnp.where(valid, mort_weight, 0.0)
    diag_pairs = jax.vmap(lambda weights, mort_list: jax.ops.segment_sum(weights, mort_list, num_segments=2 * MORT))(margin_coef * margin_coef, mort_index)
    mort_diag = STAB + unpair(diag_pairs) / 3.0

    def operate(vector):
        cells, mults = vector
        free_face = cells[0, :, :, 0].reshape(N_SPACE, FACE)
        porous_face = cells[1, :, :, CZ - 1].reshape(N_SPACE, FACE)
        rows = jax.vmap(coupling_rows)(free_face, porous_face, mort_index, face_stokes, face_darcy, margin_coef)
        free_add, porous_add = jax.vmap(coupling_cols)(pair_view(mults), mort_index, face_stokes, face_darcy, margin_coef)
        field = fine_apply(cells, active, react)
        field = field.at[0, :, :, 0].add(free_add.reshape(NX, CY))
        field = field.at[1, :, :, CZ - 1].add(porous_add.reshape(NX, CY))
        return (field, unpair(rows) - STAB * mults)

    def precondition(vector):
        return (vcycle(vector[0], active, react, fine_diag, coarse_diag), vector[1] / mort_diag)

    def inner(first, second):
        return jnp.sum(first[0] * second[0]) + jnp.sum(first[1] * second[1])
    rhs = (f_cells, g_mortar)
    lanczos_old = rhs
    lanczos_new = rhs
    work_vec = precondition(rhs)
    beta_now = jnp.sqrt(inner(rhs, work_vec))
    old_beta = jnp.zeros((), jnp.float32)
    delta_bar = jnp.zeros((), jnp.float32)
    epsilon = jnp.zeros((), jnp.float32)
    phi_bar = beta_now
    cosine = jnp.full((), -1.0, jnp.float32)
    sine_val = jnp.zeros((), jnp.float32)
    search = (jnp.zeros_like(f_cells), jnp.zeros_like(g_mortar))
    search_two = search
    solution = search
    for iteration in range(ITERS):
        basis = (work_vec[0] / beta_now, work_vec[1] / beta_now)
        image = operate(basis)
        if iteration > 0:
            image = combine(image, lanczos_old, 1.0, -(beta_now / old_beta))
        alpha_now = inner(basis, image)
        image = combine(image, lanczos_new, 1.0, -(alpha_now / beta_now))
        lanczos_old = lanczos_new
        lanczos_new = image
        work_vec = precondition(lanczos_new)
        old_beta = beta_now
        beta_now = jnp.sqrt(inner(lanczos_new, work_vec))
        old_eps, delta_val, gamma_val, phi_step, cosine, sine_val, delta_bar, epsilon, phi_bar = rotation(alpha_now, beta_now, cosine, sine_val, delta_bar, epsilon, phi_bar)
        search_one = search_two
        search_two = search
        search = ((basis[0] - old_eps * search_one[0] - delta_val * search_two[0]) / gamma_val, (basis[1] - old_eps * search_one[1] - delta_val * search_two[1]) / gamma_val)
        solution = (solution[0] + phi_step * search[0], solution[1] + phi_step * search[1])
    return (solution[0], solution[1])
```

```python
import functools

import jax
import jax.numpy as jnp
from jax import lax
from jax.experimental import pallas as pl
from jax.experimental.pallas import tpu as pltpu
from jax.sharding import PartitionSpec as P

ZONES = 16
ITERS = 4
OMEGA = 0.8
STAB = 0.05
F32 = jnp.float32
BF16 = jnp.bfloat16
MESH = pl.DeviceIdType.MESH


def radices(count):
    found = []
    while count > 1:
        step = 4 if count % 4 == 0 else (2 if count % 2 == 0 else count)
        found.append(step)
        count //= step
    return found or [1]


def kernel(
    regions,
    spaces,
    f_ref,
    g_ref,
    mask_ref,
    zone_ref,
    zcoef_ref,
    mort_ref,
    stokes_ref,
    darcy_ref,
    weight_ref,
    tiles_ref,
    x_ref,
    xm_ref,
    ar,
    act,
    diag,
    inv,
    ay,
    q,
    ae,
    ys,
    rs,
    icoarse,
    s1,
    spack,
    srecv,
    tmp,
    meta,
    metax,
    mx,
    lamx,
    lams,
    part,
    prow,
    acc,
    red,
    halo_send,
    halo_recv,
    lam_send,
    lam_recv,
    part_sem,
    red_send,
    red_recv,
):
    reg = lax.axis_index("region")
    pos = lax.axis_index("space")
    slab = f_ref.shape[1]
    ny, nz = f_ref.shape[2], f_ref.shape[3]
    nc = slab // 2
    hy = ny // 2
    mort = g_ref.shape[1]
    rows = mort_ref.shape[1]
    has_left = pos > 0
    has_right = pos < spaces - 1
    sides = ((-1, has_left), (1, has_right))
    first_region = reg == 0

    lane = lax.broadcasted_iota(jnp.int32, (ny, nz), 1)
    row = lax.broadcasted_iota(jnp.int32, (ny, nz), 0)
    layer_lane = reg * (nz - 1)
    clane = lax.broadcasted_iota(jnp.int32, (hy, nz), 1)
    crow = lax.broadcasted_iota(jnp.int32, (hy, nz), 0)
    ceven = clane % 2 == 0

    stages = []
    stride = 1
    for number, radix in enumerate(radices(spaces)):
        digit = (pos // stride) % radix
        base = pos - digit * stride
        peers = []
        for d_reg in range(regions if number == 0 else 1):
            for j in range(radix):
                if d_reg == 0 and j == 0:
                    continue
                peers.append((
                    d_reg * radix + j,
                    ((reg + d_reg) % regions, base + ((digit + j) % radix) * stride),
                ))
        stages.append(peers)
        stride *= radix

    barrier = pltpu.get_barrier_semaphore()
    waits = 0
    for peers in stages:
        for _, who in peers:
            pl.semaphore_signal(barrier, inc=1, device_id=who, device_id_type=MESH)
            waits += 1
    for step, there in sides:
        for d_reg in range(regions):
            @pl.when(there)
            def _():
                pl.semaphore_signal(
                    barrier, inc=1, device_id=((reg + d_reg) % regions, pos + step),
                    device_id_type=MESH,
                )
    beside = has_left.astype(jnp.int32) + has_right.astype(jnp.int32)
    pl.semaphore_wait(barrier, waits + regions * beside)

    def halo(kind, step, src, dst):
        side = (step + 1) // 2
        return pltpu.make_async_remote_copy(
            src_ref=src, dst_ref=dst,
            send_sem=halo_send.at[kind, side], recv_sem=halo_recv.at[kind, 1 - side],
            device_id=(reg, pos + step), device_id_type=MESH,
        )

    def start_halo(kind, src_of, dst_of):
        for step, there in sides:
            @pl.when(there)
            def _():
                halo(kind, step, src_of(step), dst_of(step)).start()

    def wait_halo(kind, src_of, dst_of):
        for step, there in sides:
            @pl.when(there)
            def _():
                halo(kind, step, src_of(step), dst_of(step)).wait_send()
                pltpu.make_async_remote_copy(
                    src_ref=src_of(-step), dst_ref=dst_of(-step),
                    send_sem=halo_send.at[kind, (1 - step) // 2],
                    recv_sem=halo_recv.at[kind, (step + 1) // 2],
                    device_id=(reg, pos + step), device_id_type=MESH,
                ).wait_recv()

    zero = jnp.zeros((ny, nz), F32)

    def clear(side_lo, there):
        @pl.when(jnp.logical_not(there))
        def _():
            for d in range(2):
                at = side_lo * (slab + 2) + d
                ar[at] = zero
                for k in range(ITERS):
                    ys[k, at] = zero
                srecv[side_lo] = jnp.zeros((hy, nz), F32)
            q[side_lo * (slab + 1)] = zero
            for k in range(3):
                metax[side_lo, k] = jnp.zeros((1, rows), F32)
            for d_reg in range(regions):
                lamx[2 * side_lo, d_reg] = jnp.zeros((1, mort), F32)

    f_src = lambda step: f_ref.at[0, pl.ds(0 if step < 0 else slab - 1, 1)]
    f_dst = lambda step: q.at[pl.ds(slab + 1 if step < 0 else 0, 1)]
    ar_src = lambda step: ar.at[pl.ds(2 if step < 0 else slab, 2)]
    ar_dst = lambda step: ar.at[pl.ds(slab + 2 if step < 0 else 0, 2)]
    meta_src = lambda step: meta
    meta_dst = lambda step: metax.at[1 if step < 0 else 0]

    def y_src(k):
        return lambda step: ys.at[k, pl.ds(2 if step < 0 else slab, 2)]

    def y_dst(k):
        return lambda step: ys.at[k, pl.ds(slab + 2 if step < 0 else 0, 2)]

    s_src = lambda step: spack.at[0 if step < 0 else 1]
    s_dst = lambda step: srecv.at[1 if step < 0 else 0]

    def react_layer(l):
        ids = zone_ref[0, l]
        value = jnp.zeros((ny, nz), F32)
        for zone in range(ZONES):
            value = jnp.where(ids == zone, zcoef_ref[zone], value)
        ar[l + 2] = jnp.where(mask_ref[0, l] != 0, value, 0.0)

    @pl.loop(0, slab)
    def _(l):
        react_layer(l)

    start_halo(1, ar_src, ar_dst)
    clear(0, has_left)
    clear(1, has_right)

    lane_row = lax.broadcasted_iota(jnp.int32, (1, rows), 1)
    limit = jnp.zeros((1, rows), jnp.int32)
    for tile in range(rows // 128):
        limit = jnp.where(lane_row // 128 == tile, tiles_ref[0, tile], limit)
    coef = jnp.where(lane_row % 128 < limit, weight_ref[...], 0.0)
    side_sign = jnp.where(first_region, 1.0, -1.0).astype(F32)
    meta[0] = mort_ref[...].astype(F32)
    meta[1] = jnp.where(first_region, stokes_ref[...], darcy_ref[...]).astype(F32)
    meta[2] = coef * side_sign
    start_halo(2, meta_src, meta_dst)
    start_halo(0, f_src, f_dst)

    @pl.loop(0, slab)
    def _(l):
        q[l + 1] = f_ref[0, l]
        rs[0, l] = f_ref[0, l]

    width = 256

    def split(value):
        high = value.astype(BF16).astype(F32)
        rest = value - high
        mid = rest.astype(BF16).astype(F32)
        return high, mid, rest - mid

    def nt_dot(a, b):
        return lax.dot_general(a, b, (((1,), (1,)), ((), ())), preferred_element_type=F32)

    multiplier = lax.broadcasted_iota(jnp.int32, (2 * mort, width), 0).astype(F32)

    def add_pairs(source, first_layer, layers, target, squares):
        face = lax.broadcasted_iota(jnp.int32, (ny, width), 0).astype(F32)
        total = jnp.zeros((8, 2 * mort), F32)
        for chunk in range(rows // width):
            span = pl.ds(chunk * width, width)
            mort_row, face_row, coef_row = (source[k, :, span] for k in range(3))
            one_hot = jnp.where(multiplier == mort_row, 1.0, 0.0).astype(BF16)
            pieces = split(coef_row)

            def body(l, carry):
                hit = face == face_row - ((first_layer + l) * ny).astype(F32)
                at = pl.ds(pl.multiple_of((target + l) * ny, ny), ny)
                value = jnp.zeros((ny, 2 * mort), F32)
                for piece in pieces:
                    value = value + nt_dot(jnp.where(hit, piece, 0.0).astype(BF16), one_hot)
                if chunk == 0:
                    mx[at, :] = value
                else:
                    mx[at, :] = mx[at, :] + value
                return carry

            lax.fori_loop(0, layers, body, 0)
            if squares:
                for piece in split(coef_row * coef_row):
                    total = total + nt_dot(
                        jnp.broadcast_to(piece, (8, width)).astype(BF16), one_hot
                    )
        return total[0:1]

    squares = add_pairs(meta, 0, slab, 1, True)
    own_half = lambda v: jnp.where(first_region, v[:, :mort], v[:, mort:])
    other_half = lambda v: jnp.where(first_region, v[:, mort:], v[:, :mort])
    inv_mort = 1.0 / (STAB + own_half(squares) / 3.0)

    wait_halo(2, meta_src, meta_dst)
    add_pairs(metax.at[0], slab - 1, 1, 0, False)
    add_pairs(metax.at[1], 0, 1, slab + 1, False)
    wait_halo(1, ar_src, ar_dst)

    @pl.loop(0, slab + 4)
    def _(l):
        act[l] = jnp.where(ar[l] > 0.0, 1.0, 0.0)

    @pl.loop(0, slab + 2)
    def _(l):
        value = jnp.where(ar[l + 1] > 0.0, 6.0 + ar[l + 1], 1.0)
        diag[l] = value
        inv[l] = OMEGA / value

    def pair_sum(total):
        tmp[...] = total
        v = tmp[pl.ds(0, hy, stride=2), :] + tmp[pl.ds(1, hy, stride=2), :]
        return v + jnp.where(ceven, pltpu.roll(v, nz - 1, 1), pltpu.roll(v, 1, 1))

    @pl.loop(0, nc + 2)
    def _(b):
        icoarse[b] = OMEGA / (12.0 + 0.25 * pair_sum(ar[2 * b] + ar[2 * b + 1]))

    def in_layer(c):
        total = jnp.where(row == 0, 0.0, pltpu.roll(c, 1, 0))
        total = total + jnp.where(row == ny - 1, 0.0, pltpu.roll(c, ny - 1, 0))
        total = total + jnp.where(lane == 0, 0.0, pltpu.roll(c, 1, 1))
        return total + jnp.where(lane == nz - 1, 0.0, pltpu.roll(c, nz - 1, 1))

    def neighbours(ref, at):
        return in_layer(ref[at]) + (ref[at - 1] + ref[at + 1])

    def coarse_in_layer(c):
        total = jnp.where(crow == 0, 0.0, pltpu.roll(c, 1, 0))
        total = total + jnp.where(crow == hy - 1, 0.0, pltpu.roll(c, hy - 1, 0))
        total = total + jnp.where(clane < 2, 0.0, pltpu.roll(c, 2, 1))
        return total + jnp.where(clane >= nz - 2, 0.0, pltpu.roll(c, nz - 2, 1))

    def scale_first(l):
        ae[l] = act[l + 1] * (inv[l] * q[l])

    def coarse_first(b):
        total = jnp.zeros((ny, nz), F32)
        for d in range(2):
            l = 2 * b + d + 1
            total = total + (0.2 * q[l] + act[l + 1] * neighbours(ae, l))
        s1[b + 2] = icoarse[b + 1] * pair_sum(total)

    def send_coarse():
        spack[0] = jnp.where(ceven, s1[2], s1[3])
        spack[1] = jnp.where(ceven, s1[nc], s1[nc + 1])
        start_halo(3, s_src, s_dst)

    def receive_coarse():
        wait_halo(3, s_src, s_dst)
        for side, at in ((0, 0), (1, nc + 2)):
            v = srecv[side]
            s1[at] = jnp.where(ceven, v, pltpu.roll(v, 1, 1))
            s1[at + 1] = jnp.where(ceven, pltpu.roll(v, nz - 1, 1), v)

    def second_block(b):
        s2 = 1.2 * s1[b + 1] + 2.0 * icoarse[b] * (
            coarse_in_layer(s1[b + 1]) + (s1[b] + s1[b + 2])
        )
        tmp[pl.ds(0, hy, stride=2), :] = s2
        tmp[pl.ds(1, hy, stride=2), :] = s2
        return tmp[...]

    e2 = ay

    def second_all():
        up = second_block(0)
        e2[0] = inv[0] * q[0] + up
        ae[0] = act[1] * e2[0]
        up = second_block(nc + 1)
        e2[slab + 1] = inv[slab + 1] * q[slab + 1] + up
        ae[slab + 1] = act[slab + 2] * e2[slab + 1]

        @pl.loop(1, nc + 1)
        def _(b):
            up = second_block(b)
            for d in range(2):
                l = 2 * b - 1 + d
                value = inv[l] * q[l] + up
                e2[l] = value
                ae[l] = act[l + 1] * value

    def last_layer(l):
        return 0.2 * e2[l] + inv[l] * (q[l] + act[l + 1] * neighbours(ae, l))

    def fold(v):
        out = v[:, 0:128]
        for k in range(1, v.shape[1] // 128):
            out = out + v[:, 128 * k : 128 * (k + 1)]
        return out

    def lay_sum(v):
        return jnp.sum(v.reshape(ny // 8, 8, nz), axis=0)

    def red_copy(parity, number, slot, who):
        return pltpu.make_async_remote_copy(
            src_ref=acc.at[parity, number], dst_ref=red.at[parity, number, slot],
            send_sem=red_send.at[parity, number, slot],
            recv_sem=red_recv.at[parity, number, slot],
            device_id=who, device_id_type=MESH,
        )

    def red_start(parity, number):
        for slot, who in stages[number]:
            red_copy(parity, number, slot, who).start()

    def red_wait(parity, number):
        for slot, who in stages[number]:
            red_copy(parity, number, slot, who).wait()
        total = acc[parity, number]
        for slot, _ in stages[number]:
            total = total + red[parity, number, slot]
        return total

    def red_next(parity, number):
        acc[parity, number + 1] = red_wait(parity, number)
        red_start(parity, number + 1)

    last_stage = len(stages) - 1

    def lam_copy(k, step, d_reg, sending):
        there = step if sending else -step
        return pltpu.make_async_remote_copy(
            src_ref=lams.at[k], dst_ref=lamx.at[1 - there, d_reg],
            send_sem=lam_send.at[there + 1, d_reg], recv_sem=lam_recv.at[1 - there, d_reg],
            device_id=((reg + d_reg) % regions, pos + step), device_id_type=MESH,
        )

    def lam_each(action):
        for step, there in ((-1, has_left), (0, None), (1, has_right)):
            for d_reg in range(regions):
                if step == 0:
                    if d_reg:
                        action(step, d_reg)
                else:
                    pl.when(there)(functools.partial(action, step, d_reg))

    def lam_start(k):
        lam_each(lambda step, d_reg: lam_copy(k, step, d_reg, True).start())

    def lam_wait(k):
        def both(step, d_reg):
            lam_copy(k, step, d_reg, True).wait_send()
            lam_copy(k, step, d_reg, False).wait_recv()

        lam_each(both)

    def paired(offset, own):
        mine, others = own, lamx[offset, 1]
        return jnp.concatenate(
            [jnp.where(first_region, mine, others), jnp.where(first_region, others, mine)], axis=1
        )

    def apply_cells(k, l):
        y = ys[k, l + 1]
        q[l] = diag[l] * y - act[l + 1] * neighbours(ay, l + 1)

    def add_face(l, lam_row):
        at = pl.ds(l * ny if isinstance(l, int) else pl.multiple_of(l * ny, ny), ny)
        col = jnp.sum(mx[at, :] * lam_row, axis=1, keepdims=True)
        q[l] = q[l] + jnp.where(lane == layer_lane, col, 0.0)

    wait_halo(0, f_src, f_dst)

    @pl.loop(0, slab + 2)
    def _(l):
        scale_first(l)

    @pl.loop(0, nc)
    def _(b):
        coarse_first(b)

    send_coarse()
    res_m = [g_ref[...]]
    lam = g_ref[...] * inv_mort
    lams[0] = lam
    lam_start(0)
    receive_coarse()
    second_all()

    one = jnp.ones((1, 1), F32)
    mults = [lam]
    beta_prev = None
    ry_local = None
    coefs_old, coefs_new, coefs_x = [], [], []
    cosine, sine = -one, 0.0 * one
    delta_bar, epsilon = 0.0 * one, 0.0 * one
    phi_bar = None

    def out_pass(k, scales):
        def body(l, total):
            value = last_layer(l + 1)
            if scales is None:
                resid = rs[0, l]
            else:
                s_q, s_old, s_now = scales
                value = s_q * value - s_now * ys[k - 1, l + 2]
                resid = s_q * q[l + 1] - s_now * rs[(k - 1) % 3, l]
                if s_old is not None:
                    value = value - s_old * ys[k - 2, l + 2]
                    resid = resid - s_old * rs[(k - 2) % 3, l]
                rs[k % 3, l] = resid
            ys[k, l + 2] = value
            return total + lay_sum(value * resid)

        total = jnp.zeros((8, nz), F32)
        total = lax.fori_loop(0, 2, body, total)
        total = lax.fori_loop(slab - 2, slab, body, total)
        if k < ITERS:
            start_halo(4, y_src(k), y_dst(k))
        total = lax.fori_loop(2, slab - 2, body, total)
        return jnp.sum(total, axis=0, keepdims=True)

    ry_local = out_pass(0, None) + fold(lam * res_m[0])
    for k in range(ITERS):
        parity = k % 2
        lam = mults[k]

        @pl.loop(2, slab + 2)
        def _(l):
            ay[l] = act[l] * ys[k, l]

        lam_wait(k)
        own_pair = paired(1, lam)

        def operate(l, carry):
            apply_cells(k, l)
            add_face(l, own_pair)
            y = ys[k, l + 1]
            u = jnp.where(first_region, y[:, 0:1], y[:, nz - 1 : nz])
            at = pl.ds(pl.multiple_of(l * ny, ny), ny)
            prod, old, prt = carry
            prod = prod + lay_sum(y * q[l])
            if k > 0:
                old = old + lay_sum(y * rs[(k - 1) % 3, l - 1])
            prt = prt + jnp.sum((mx[at, :] * u).reshape(ny // 8, 8, 2 * mort), axis=0)
            scale_first(l)
            return prod, old, prt

        carry = (
            jnp.zeros((8, nz), F32),
            jnp.zeros((8, nz), F32),
            jnp.zeros((8, 2 * mort), F32),
        )
        carry = lax.fori_loop(2, slab, operate, carry)

        @pl.loop(1, nc - 1)
        def _(b):
            coarse_first(b)

        wait_halo(4, y_src(k), y_dst(k))
        for l in (0, 1, slab + 2, slab + 3):
            ay[l] = act[l] * ys[k, l]
        carry = operate(jnp.int32(1), carry)
        prod, old, prt = operate(jnp.int32(slab), carry)
        apply_cells(k, 0)
        apply_cells(k, slab + 1)
        add_face(0, paired(0, lamx[0, 0]))
        add_face(slab + 1, paired(2, lamx[2, 0]))
        scale_first(0)
        scale_first(slab + 1)
        coarse_first(0)
        coarse_first(nc - 1)
        send_coarse()
        partial_rows = jnp.sum(prt, axis=0, keepdims=True)
        prow[...] = other_half(partial_rows)
        part_copy = pltpu.make_async_remote_copy(
            src_ref=prow, dst_ref=part, send_sem=part_sem.at[0], recv_sem=part_sem.at[1],
            device_id=((reg + 1) % regions, pos), device_id_type=MESH,
        )
        part_copy.start()
        prod_row = jnp.sum(prod, axis=0, keepdims=True)
        prod_row = prod_row + fold(own_pair * partial_rows) - STAB * fold(lam * lam)
        old_row = jnp.sum(old, axis=0, keepdims=True)
        if k > 0:
            old_row = old_row + fold(lam * res_m[k - 1])
        acc[parity, 0, 0:1] = ry_local
        acc[parity, 0, 1:2] = prod_row
        acc[parity, 0, 2:3] = old_row
        acc[parity, 0, 3:8] = jnp.zeros((5, 128), F32)
        red_start(parity, 0)
        receive_coarse()
        for number in range(last_stage):
            red_next(parity, number)
        part_copy.wait()
        q_m = own_half(partial_rows) + part[...] - STAB * lam
        second_all()
        total = red_wait(parity, last_stage)
        sums = jnp.sum(total, axis=1, keepdims=True)
        ry, yky, yr = sums[0:1], sums[1:2], sums[2:3]
        beta = jnp.sqrt(ry)
        alpha = yky / ry
        if k > 0:
            alpha = alpha - yr / beta_prev
        def rotate(alpha_now, beta_next, column):
            nonlocal cosine, sine, delta_bar, epsilon, phi_bar
            nonlocal coefs_old, coefs_new, coefs_x
            old_eps = epsilon
            delta = cosine * delta_bar + sine * alpha_now
            gamma_bar = sine * delta_bar - cosine * alpha_now
            epsilon = sine * beta_next
            delta_bar = -cosine * beta_next
            gamma = jnp.sqrt(gamma_bar * gamma_bar + beta_next * beta_next)
            cosine = gamma_bar / gamma
            sine = beta_next / gamma
            phi = cosine * phi_bar
            phi_bar = sine * phi_bar
            now = []
            for i in range(column + 1):
                value = 1.0 / betas[i] if i == column else 0.0 * one
                if i < len(coefs_old):
                    value = value - old_eps * coefs_old[i]
                if i < len(coefs_new):
                    value = value - delta * coefs_new[i]
                now.append(value / gamma)
            coefs_old, coefs_new = coefs_new, now
            coefs_x = [
                (coefs_x[i] if i < len(coefs_x) else 0.0) + phi * now[i]
                for i in range(column + 1)
            ]

        if k == 0:
            phi_bar = beta
            betas = [beta]
        else:
            betas.append(beta)
            rotate(alpha_prev, beta, k - 1)
        scales = (1.0 / beta, None if k == 0 else beta / beta_prev, alpha / beta)
        next_res = scales[0] * q_m - scales[2] * res_m[k]
        next_lam = scales[0] * (q_m * inv_mort) - scales[2] * lam
        if k > 0:
            next_res = next_res - scales[1] * res_m[k - 1]
            next_lam = next_lam - scales[1] * mults[k - 1]
        res_m.append(next_res)
        mults.append(next_lam)
        if k + 1 < ITERS:
            lams[k + 1] = next_lam
            lam_start(k + 1)
        ry_local = out_pass(k + 1, scales) + fold(next_lam * next_res)
        beta_prev, alpha_prev = beta, alpha

    parity = ITERS % 2
    acc[parity, 0, 0:1] = ry_local
    acc[parity, 0, 1:8] = jnp.zeros((7, 128), F32)
    red_start(parity, 0)
    for number in range(last_stage):
        red_next(parity, number)
    total = red_wait(parity, last_stage)
    rotate(alpha_prev, jnp.sqrt(jnp.sum(total[0:1], axis=1, keepdims=True)), ITERS - 1)

    @pl.loop(0, slab)
    def _(l):
        value = coefs_x[0] * ys[0, l + 2]
        for k in range(1, ITERS):
            value = value + coefs_x[k] * ys[k, l + 2]
        x_ref[0, l] = value

    value = coefs_x[0] * mults[0]
    for k in range(1, ITERS):
        value = value + coefs_x[k] * mults[k]
    xm_ref[...] = value


def on_device(regions, spaces, *args):
    f_cells, g_mortar, rows = args[0], args[1], args[5].shape[1]
    slab, ny, nz = f_cells.shape[1:]
    mort = g_mortar.shape[1]
    steps = radices(spaces)
    slots = max([regions * steps[0]] + steps)
    vmem = pl.BlockSpec(memory_space=pltpu.VMEM)
    smem = pl.BlockSpec(memory_space=pltpu.SMEM)
    field = lambda *lead: pltpu.VMEM(lead + (ny, nz), F32)
    coarse = lambda *lead: pltpu.VMEM(lead + (ny // 2, nz), F32)
    dma = lambda *shape: pltpu.SemaphoreType.DMA(shape)
    return pl.pallas_call(
        functools.partial(kernel, regions, spaces),
        out_shape=(
            jax.ShapeDtypeStruct(f_cells.shape, F32),
            jax.ShapeDtypeStruct(g_mortar.shape, F32),
        ),
        in_specs=[vmem] * 4 + [smem] + [vmem] * 4 + [smem],
        out_specs=(vmem, vmem),
        scratch_shapes=[
            field(slab + 4),
            field(slab + 4),
            field(slab + 2),
            field(slab + 2),
            field(slab + 4),
            field(slab + 2),
            field(slab + 2),
            field(ITERS + 1, slab + 4),
            field(3, slab),
            coarse(slab // 2 + 2),
            coarse(slab // 2 + 4),
            coarse(2),
            coarse(2),
            field(),
            pltpu.VMEM((3, 1, rows), F32),
            pltpu.VMEM((2, 3, 1, rows), F32),
            pltpu.VMEM(((slab + 2) * ny, 2 * mort), F32),
            pltpu.VMEM((3, regions, 1, mort), F32),
            pltpu.VMEM((ITERS, 1, mort), F32),
            pltpu.VMEM((1, mort), F32),
            pltpu.VMEM((1, mort), F32),
            pltpu.VMEM((2, len(steps), 8, 128), F32),
            pltpu.VMEM((2, len(steps), slots, 8, 128), F32),
            dma(5, 2),
            dma(5, 2),
            dma(3, regions),
            dma(3, regions),
            dma(2),
            dma(2, len(steps), slots),
            dma(2, len(steps), slots),
        ],
        compiler_params=pltpu.CompilerParams(
            collective_id=0, has_side_effects=True, vmem_limit_bytes=48 * 1024 * 1024
        ),
    )(*args)


def solution(mesh):
    in_specs = (
        P("region", "space", None, None),
        P("region", "space"),
        P("region", "space", None, None),
        P("region", "space", None, None),
        P(),
        P("space", None),
        P("space", None),
        P("space", None),
        P("space", None),
        P("space", None),
    )
    out_specs = (P("region", "space", None, None), P("region", "space"))
    return jax.shard_map(
        functools.partial(on_device, mesh.shape["region"], mesh.shape["space"]),
        mesh=mesh, in_specs=in_specs, out_specs=out_specs, check_vma=False,
    )
```

```python
import functools

import jax
import jax.numpy as jnp
from jax import lax
from jax.experimental import pallas as pl
from jax.experimental.pallas import tpu as pltpu
from jax.sharding import PartitionSpec as P

ZONES = 16
ITERS = 4
OMEGA = 0.8
STAB = 0.05
F32 = jnp.float32
BF16 = jnp.bfloat16
MESH = pl.DeviceIdType.MESH


def radices(count):
    found = []
    while count > 1:
        step = 4 if count % 4 == 0 else (2 if count % 2 == 0 else count)
        found.append(step)
        count //= step
    return found or [1]


def kernel(
    regions,
    spaces,
    f_hbm,
    g_hbm,
    mask_hbm,
    zone_hbm,
    zcoef_ref,
    mort_hbm,
    stokes_hbm,
    darcy_hbm,
    weight_hbm,
    tiles_ref,
    x_ref,
    xm_ref,
    f_ref,
    g_ref,
    mask_ref,
    zone_ref,
    mort_ref,
    stokes_ref,
    darcy_ref,
    weight_ref,
    in_sem,
    one_hot,
    lhs,
    ar,
    act,
    diag,
    inv,
    ay,
    q,
    ae,
    ys,
    rs,
    icoarse,
    s1,
    spack,
    srecv,
    tmp,
    meta,
    metax,
    mx,
    lamx,
    lams,
    part,
    prow,
    acc,
    red,
    halo_send,
    halo_recv,
    lam_send,
    lam_recv,
    part_sem,
    red_send,
    red_recv,
):
    copies = [
        pltpu.make_async_copy(src, dst, in_sem.at[i])
        for i, (src, dst) in enumerate((
            (mask_hbm, mask_ref),
            (zone_hbm, zone_ref),
            (f_hbm, f_ref),
            (g_hbm, g_ref),
            (mort_hbm, mort_ref),
            (stokes_hbm, stokes_ref),
            (darcy_hbm, darcy_ref),
            (weight_hbm, weight_ref),
        ))
    ]
    for copy in copies:
        copy.start()
    reg = lax.axis_index("region")
    pos = lax.axis_index("space")
    slab = f_ref.shape[1]
    ny, nz = f_ref.shape[2], f_ref.shape[3]
    nc = slab // 2
    hy = ny // 2
    mort = g_ref.shape[1]
    rows = mort_ref.shape[1]
    has_left = pos > 0
    has_right = pos < spaces - 1
    sides = ((-1, has_left), (1, has_right))
    first_region = reg == 0

    lane = lax.broadcasted_iota(jnp.int32, (ny, nz), 1)
    row = lax.broadcasted_iota(jnp.int32, (ny, nz), 0)
    layer_lane = reg * (nz - 1)
    clane = lax.broadcasted_iota(jnp.int32, (hy, nz), 1)
    crow = lax.broadcasted_iota(jnp.int32, (hy, nz), 0)
    ceven = clane % 2 == 0

    stages = []
    stride = 1
    for number, radix in enumerate(radices(spaces)):
        digit = (pos // stride) % radix
        base = pos - digit * stride
        peers = []
        for d_reg in range(regions if number == 0 else 1):
            for j in range(radix):
                if d_reg == 0 and j == 0:
                    continue
                peers.append((
                    d_reg * radix + j,
                    ((reg + d_reg) % regions, base + ((digit + j) % radix) * stride),
                ))
        stages.append(peers)
        stride *= radix

    barrier = pltpu.get_barrier_semaphore()
    waits = 0
    for peers in stages:
        for _, who in peers:
            pl.semaphore_signal(barrier, inc=1, device_id=who, device_id_type=MESH)
            waits += 1
    for step, there in sides:
        for d_reg in range(regions):
            @pl.when(there)
            def _():
                pl.semaphore_signal(
                    barrier, inc=1, device_id=((reg + d_reg) % regions, pos + step),
                    device_id_type=MESH,
                )
    beside = has_left.astype(jnp.int32) + has_right.astype(jnp.int32)
    pl.semaphore_wait(barrier, waits + regions * beside)

    def halo(kind, step, src, dst):
        side = (step + 1) // 2
        return pltpu.make_async_remote_copy(
            src_ref=src, dst_ref=dst,
            send_sem=halo_send.at[kind, side], recv_sem=halo_recv.at[kind, 1 - side],
            device_id=(reg, pos + step), device_id_type=MESH,
        )

    def start_halo(kind, src_of, dst_of):
        for step, there in sides:
            @pl.when(there)
            def _():
                halo(kind, step, src_of(step), dst_of(step)).start()

    def wait_halo(kind, src_of, dst_of):
        for step, there in sides:
            @pl.when(there)
            def _():
                halo(kind, step, src_of(step), dst_of(step)).wait_send()
                pltpu.make_async_remote_copy(
                    src_ref=src_of(-step), dst_ref=dst_of(-step),
                    send_sem=halo_send.at[kind, (1 - step) // 2],
                    recv_sem=halo_recv.at[kind, (step + 1) // 2],
                    device_id=(reg, pos + step), device_id_type=MESH,
                ).wait_recv()

    zero = jnp.zeros((ny, nz), F32)

    def clear(side_lo, there):
        @pl.when(jnp.logical_not(there))
        def _():
            for d in range(2):
                at = side_lo * (slab + 2) + d
                ar[at] = zero
                for k in range(ITERS):
                    ys[k, at] = zero
                srecv[side_lo] = jnp.zeros((hy, nz), F32)
            q[side_lo * (slab + 1)] = zero
            for k in range(3):
                metax[side_lo, k] = jnp.zeros((1, rows), F32)
            for d_reg in range(regions):
                lamx[2 * side_lo, d_reg] = jnp.zeros((1, mort), F32)

    f_src = lambda step: f_ref.at[0, pl.ds(0 if step < 0 else slab - 1, 1)]
    f_dst = lambda step: q.at[pl.ds(slab + 1 if step < 0 else 0, 1)]
    ar_src = lambda step: ar.at[pl.ds(2 if step < 0 else slab, 2)]
    ar_dst = lambda step: ar.at[pl.ds(slab + 2 if step < 0 else 0, 2)]
    meta_src = lambda step: meta
    meta_dst = lambda step: metax.at[1 if step < 0 else 0]

    def y_src(k):
        return lambda step: ys.at[k, pl.ds(2 if step < 0 else slab, 2)]

    def y_dst(k):
        return lambda step: ys.at[k, pl.ds(slab + 2 if step < 0 else 0, 2)]

    s_src = lambda step: spack.at[0 if step < 0 else 1]
    s_dst = lambda step: srecv.at[1 if step < 0 else 0]

    def react_layer(l):
        ids = zone_ref[0, l]
        value = jnp.zeros((ny, nz), F32)
        for zone in range(ZONES):
            value = jnp.where(ids == zone, zcoef_ref[zone], value)
        ar[l + 2] = jnp.where(mask_ref[0, l] != 0, value, 0.0)

    for copy in copies:
        copy.wait()

    @pl.loop(0, slab)
    def _(l):
        react_layer(l)

    start_halo(1, ar_src, ar_dst)
    clear(0, has_left)
    clear(1, has_right)

    lane_row = lax.broadcasted_iota(jnp.int32, (1, rows), 1)
    limit = jnp.zeros((1, rows), jnp.int32)
    for tile in range(rows // 128):
        limit = jnp.where(lane_row // 128 == tile, tiles_ref[0, tile], limit)
    coef = jnp.where(lane_row % 128 < limit, weight_ref[...], 0.0)
    side_sign = jnp.where(first_region, 1.0, -1.0).astype(F32)
    meta[0] = mort_ref[...].astype(F32)
    meta[1] = jnp.where(first_region, stokes_ref[...], darcy_ref[...]).astype(F32)
    meta[2] = coef * side_sign
    start_halo(2, meta_src, meta_dst)
    start_halo(0, f_src, f_dst)

    @pl.loop(0, slab)
    def _(l):
        q[l + 1] = f_ref[0, l]
        rs[0, l] = f_ref[0, l]

    def split(value):
        high = value.astype(BF16).astype(F32)
        rest = value - high
        mid = rest.astype(BF16).astype(F32)
        return high, mid, rest - mid

    face = lax.broadcasted_iota(jnp.int32, (ny, rows), 0).astype(F32)
    multiplier = lax.broadcasted_iota(jnp.int32, (128, 2 * mort), 1).astype(F32)

    def set_one_hot(source):
        tiles = rows // 128
        listed = [source[0, :, pl.ds(128 * t, 128)] for t in range(tiles)]
        listed.append(jnp.zeros((128 - tiles, 128), F32))
        down = jnp.transpose(jnp.concatenate(listed, axis=0))
        for t in range(tiles):
            hit = multiplier == down[:, t : t + 1]
            one_hot[pl.ds(128 * t, 128), :] = jnp.where(hit, 1.0, 0.0).astype(BF16)

    def set_layers(source, first_layer, layers, target):
        face_row, coef_row = source[1], source[2]
        high, mid, _ = split(coef_row)
        for i in range(layers):
            start = jnp.asarray((first_layer + i) * ny, jnp.int32).astype(F32)
            hit = face == face_row - start
            lhs[pl.ds(2 * i * ny, ny), :] = jnp.where(hit, high, 0.0).astype(BF16)
            lhs[pl.ds((2 * i + 1) * ny, ny), :] = jnp.where(hit, mid, 0.0).astype(BF16)
        value = jnp.dot(
            lhs[pl.ds(0, 2 * layers * ny), :], one_hot[...], preferred_element_type=F32
        )
        for i in range(layers):
            at = (target + i) * ny
            at = pl.ds(at if isinstance(at, int) else pl.multiple_of(at, ny), ny)
            mx[at, :] = value[2 * i * ny : (2 * i + 1) * ny] + value[
                (2 * i + 1) * ny : (2 * i + 2) * ny
            ]

    set_one_hot(meta)

    @pl.loop(0, slab // 2)
    def _(pair):
        set_layers(meta, 2 * pair, 2, 1 + 2 * pair)

    high, mid, low = split(meta[2] * meta[2])
    piece = lax.broadcasted_iota(jnp.int32, (16, rows), 0)
    pieces = jnp.where(
        piece == 0, high, jnp.where(piece == 1, mid, jnp.where(piece == 2, low, 0.0))
    )
    squares = jnp.sum(
        jnp.dot(pieces.astype(BF16), one_hot[...], preferred_element_type=F32),
        axis=0, keepdims=True,
    )
    own_half = lambda v: jnp.where(first_region, v[:, :mort], v[:, mort:])
    other_half = lambda v: jnp.where(first_region, v[:, mort:], v[:, :mort])
    inv_mort = 1.0 / (STAB + own_half(squares) / 3.0)

    wait_halo(2, meta_src, meta_dst)
    set_one_hot(metax.at[0])
    set_layers(metax.at[0], slab - 1, 1, 0)
    set_one_hot(metax.at[1])
    set_layers(metax.at[1], 0, 1, slab + 1)
    wait_halo(1, ar_src, ar_dst)

    @pl.loop(0, slab + 4)
    def _(l):
        act[l] = jnp.where(ar[l] > 0.0, 1.0, 0.0)

    @pl.loop(0, slab + 2)
    def _(l):
        value = jnp.where(ar[l + 1] > 0.0, 6.0 + ar[l + 1], 1.0)
        diag[l] = value
        inv[l] = OMEGA / value

    def pair_sum(total):
        tmp[...] = total
        v = tmp[pl.ds(0, hy, stride=2), :] + tmp[pl.ds(1, hy, stride=2), :]
        return v + jnp.where(ceven, pltpu.roll(v, nz - 1, 1), pltpu.roll(v, 1, 1))

    @pl.loop(0, nc + 2)
    def _(b):
        icoarse[b] = OMEGA / (12.0 + 0.25 * pair_sum(ar[2 * b] + ar[2 * b + 1]))

    def in_layer(c):
        total = jnp.where(row == 0, 0.0, pltpu.roll(c, 1, 0))
        total = total + jnp.where(row == ny - 1, 0.0, pltpu.roll(c, ny - 1, 0))
        total = total + jnp.where(lane == 0, 0.0, pltpu.roll(c, 1, 1))
        return total + jnp.where(lane == nz - 1, 0.0, pltpu.roll(c, nz - 1, 1))

    def neighbours(ref, at):
        return in_layer(ref[at]) + (ref[at - 1] + ref[at + 1])

    def coarse_in_layer(c):
        total = jnp.where(crow == 0, 0.0, pltpu.roll(c, 1, 0))
        total = total + jnp.where(crow == hy - 1, 0.0, pltpu.roll(c, hy - 1, 0))
        total = total + jnp.where(clane < 2, 0.0, pltpu.roll(c, 2, 1))
        return total + jnp.where(clane >= nz - 2, 0.0, pltpu.roll(c, nz - 2, 1))

    def scale_first(l):
        ae[l] = act[l + 1] * (inv[l] * q[l])

    def coarse_first(b):
        total = jnp.zeros((ny, nz), F32)
        for d in range(2):
            l = 2 * b + d + 1
            total = total + (0.2 * q[l] + act[l + 1] * neighbours(ae, l))
        s1[b + 2] = icoarse[b + 1] * pair_sum(total)

    def send_coarse():
        spack[0] = jnp.where(ceven, s1[2], s1[3])
        spack[1] = jnp.where(ceven, s1[nc], s1[nc + 1])
        start_halo(3, s_src, s_dst)

    def receive_coarse():
        wait_halo(3, s_src, s_dst)
        for side, at in ((0, 0), (1, nc + 2)):
            v = srecv[side]
            s1[at] = jnp.where(ceven, v, pltpu.roll(v, 1, 1))
            s1[at + 1] = jnp.where(ceven, pltpu.roll(v, nz - 1, 1), v)

    def second_block(b):
        s2 = 1.2 * s1[b + 1] + 2.0 * icoarse[b] * (
            coarse_in_layer(s1[b + 1]) + (s1[b] + s1[b + 2])
        )
        tmp[pl.ds(0, hy, stride=2), :] = s2
        tmp[pl.ds(1, hy, stride=2), :] = s2
        return tmp[...]

    e2 = ay

    def second_all():
        up = second_block(0)
        e2[0] = inv[0] * q[0] + up
        ae[0] = act[1] * e2[0]
        up = second_block(nc + 1)
        e2[slab + 1] = inv[slab + 1] * q[slab + 1] + up
        ae[slab + 1] = act[slab + 2] * e2[slab + 1]

        @pl.loop(1, nc + 1)
        def _(b):
            up = second_block(b)
            for d in range(2):
                l = 2 * b - 1 + d
                value = inv[l] * q[l] + up
                e2[l] = value
                ae[l] = act[l + 1] * value

    def last_layer(l):
        return 0.2 * e2[l] + inv[l] * (q[l] + act[l + 1] * neighbours(ae, l))

    def finish_image():
        @pl.loop(1, slab + 1)
        def _(l):
            e2[l] = last_layer(l)

    def fold(v):
        out = v[:, 0:128]
        for k in range(1, v.shape[1] // 128):
            out = out + v[:, 128 * k : 128 * (k + 1)]
        return out

    def lay_sum(v):
        return jnp.sum(v.reshape(ny // 8, 8, nz), axis=0)

    def red_copy(parity, number, slot, who):
        return pltpu.make_async_remote_copy(
            src_ref=acc.at[parity, number], dst_ref=red.at[parity, number, slot],
            send_sem=red_send.at[parity, number, slot],
            recv_sem=red_recv.at[parity, number, slot],
            device_id=who, device_id_type=MESH,
        )

    def red_start(parity, number):
        for slot, who in stages[number]:
            red_copy(parity, number, slot, who).start()

    def red_wait(parity, number):
        for slot, who in stages[number]:
            red_copy(parity, number, slot, who).wait()
        total = acc[parity, number]
        for slot, _ in stages[number]:
            total = total + red[parity, number, slot]
        return total

    def red_next(parity, number):
        acc[parity, number + 1] = red_wait(parity, number)
        red_start(parity, number + 1)

    last_stage = len(stages) - 1

    def lam_copy(k, step, d_reg, sending):
        there = step if sending else -step
        return pltpu.make_async_remote_copy(
            src_ref=lams.at[k], dst_ref=lamx.at[1 - there, d_reg],
            send_sem=lam_send.at[there + 1, d_reg], recv_sem=lam_recv.at[1 - there, d_reg],
            device_id=((reg + d_reg) % regions, pos + step), device_id_type=MESH,
        )

    def lam_each(action):
        for step, there in ((-1, has_left), (0, None), (1, has_right)):
            for d_reg in range(regions):
                if step == 0:
                    if d_reg:
                        action(step, d_reg)
                else:
                    pl.when(there)(functools.partial(action, step, d_reg))

    def lam_start(k):
        lam_each(lambda step, d_reg: lam_copy(k, step, d_reg, True).start())

    def lam_wait(k):
        def both(step, d_reg):
            lam_copy(k, step, d_reg, True).wait_send()
            lam_copy(k, step, d_reg, False).wait_recv()

        lam_each(both)

    def paired(offset, own):
        mine, others = own, lamx[offset, 1]
        return jnp.concatenate(
            [jnp.where(first_region, mine, others), jnp.where(first_region, others, mine)], axis=1
        )

    def apply_cells(k, l):
        y = ys[k, l + 1]
        q[l] = diag[l] * y - act[l + 1] * neighbours(ay, l + 1)

    def add_face(l, lam_row):
        at = pl.ds(l * ny if isinstance(l, int) else pl.multiple_of(l * ny, ny), ny)
        col = jnp.sum(mx[at, :] * lam_row, axis=1, keepdims=True)
        q[l] = q[l] + jnp.where(lane == layer_lane, col, 0.0)

    wait_halo(0, f_src, f_dst)

    @pl.loop(0, slab + 2)
    def _(l):
        scale_first(l)

    @pl.loop(0, nc)
    def _(b):
        coarse_first(b)

    send_coarse()
    res_m = [g_ref[...]]
    lam = g_ref[...] * inv_mort
    lams[0] = lam
    lam_start(0)
    receive_coarse()
    second_all()
    finish_image()

    one = jnp.ones((1, 1), F32)
    mults = [lam]
    beta_prev = None
    ry_local = None
    coefs_old, coefs_new, coefs_x = [], [], []
    cosine, sine = -one, 0.0 * one
    delta_bar, epsilon = 0.0 * one, 0.0 * one
    phi_bar = None

    def out_pass(k, scales):
        def body(l, total):
            value = e2[l + 1]
            if scales is None:
                resid = rs[0, l]
            else:
                s_q, s_old, s_now = scales
                value = s_q * value - s_now * ys[k - 1, l + 2]
                resid = s_q * q[l + 1] - s_now * rs[(k - 1) % 3, l]
                if s_old is not None:
                    value = value - s_old * ys[k - 2, l + 2]
                    resid = resid - s_old * rs[(k - 2) % 3, l]
                rs[k % 3, l] = resid
            ys[k, l + 2] = value
            return total + lay_sum(value * resid)

        total = jnp.zeros((8, nz), F32)
        total = lax.fori_loop(0, 2, body, total)
        total = lax.fori_loop(slab - 2, slab, body, total)
        if k < ITERS:
            start_halo(4, y_src(k), y_dst(k))
        total = lax.fori_loop(2, slab - 2, body, total)
        return jnp.sum(total, axis=0, keepdims=True)

    ry_local = out_pass(0, None) + fold(lam * res_m[0])
    for k in range(ITERS):
        parity = k % 2
        lam = mults[k]

        @pl.loop(2, slab + 2)
        def _(l):
            ay[l] = act[l] * ys[k, l]

        lam_wait(k)
        own_pair = paired(1, lam)

        def operate(l, carry):
            apply_cells(k, l)
            add_face(l, own_pair)
            y = ys[k, l + 1]
            u = jnp.where(first_region, y[:, 0:1], y[:, nz - 1 : nz])
            at = pl.ds(pl.multiple_of(l * ny, ny), ny)
            prod, old, prt = carry
            prod = prod + lay_sum(y * q[l])
            if k > 0:
                old = old + lay_sum(y * rs[(k - 1) % 3, l - 1])
            prt = prt + jnp.sum((mx[at, :] * u).reshape(ny // 8, 8, 2 * mort), axis=0)
            scale_first(l)
            return prod, old, prt

        carry = (
            jnp.zeros((8, nz), F32),
            jnp.zeros((8, nz), F32),
            jnp.zeros((8, 2 * mort), F32),
        )
        carry = lax.fori_loop(2, slab, operate, carry)

        @pl.loop(1, nc - 1)
        def _(b):
            coarse_first(b)

        wait_halo(4, y_src(k), y_dst(k))
        for l in (0, 1, slab + 2, slab + 3):
            ay[l] = act[l] * ys[k, l]
        carry = operate(jnp.int32(1), carry)
        prod, old, prt = operate(jnp.int32(slab), carry)
        apply_cells(k, 0)
        apply_cells(k, slab + 1)
        add_face(0, paired(0, lamx[0, 0]))
        add_face(slab + 1, paired(2, lamx[2, 0]))
        scale_first(0)
        scale_first(slab + 1)
        coarse_first(0)
        coarse_first(nc - 1)
        send_coarse()
        partial_rows = jnp.sum(prt, axis=0, keepdims=True)
        prow[...] = other_half(partial_rows)
        part_copy = pltpu.make_async_remote_copy(
            src_ref=prow, dst_ref=part, send_sem=part_sem.at[0], recv_sem=part_sem.at[1],
            device_id=((reg + 1) % regions, pos), device_id_type=MESH,
        )
        part_copy.start()
        prod_row = jnp.sum(prod, axis=0, keepdims=True)
        prod_row = prod_row + fold(own_pair * partial_rows) - STAB * fold(lam * lam)
        old_row = jnp.sum(old, axis=0, keepdims=True)
        if k > 0:
            old_row = old_row + fold(lam * res_m[k - 1])
        acc[parity, 0, 0:1] = ry_local
        acc[parity, 0, 1:2] = prod_row
        acc[parity, 0, 2:3] = old_row
        acc[parity, 0, 3:8] = jnp.zeros((5, 128), F32)
        red_start(parity, 0)
        for number in range(last_stage):
            red_next(parity, number)
        receive_coarse()
        part_copy.wait()
        q_m = own_half(partial_rows) + part[...] - STAB * lam
        second_all()
        finish_image()
        total = red_wait(parity, last_stage)
        sums = jnp.sum(total, axis=1, keepdims=True)
        ry, yky, yr = sums[0:1], sums[1:2], sums[2:3]
        beta = jnp.sqrt(ry)
        alpha = yky / ry
        if k > 0:
            alpha = alpha - yr / beta_prev
        def rotate(alpha_now, beta_next, column):
            nonlocal cosine, sine, delta_bar, epsilon, phi_bar
            nonlocal coefs_old, coefs_new, coefs_x
            old_eps = epsilon
            delta = cosine * delta_bar + sine * alpha_now
            gamma_bar = sine * delta_bar - cosine * alpha_now
            epsilon = sine * beta_next
            delta_bar = -cosine * beta_next
            gamma = jnp.sqrt(gamma_bar * gamma_bar + beta_next * beta_next)
            cosine = gamma_bar / gamma
            sine = beta_next / gamma
            phi = cosine * phi_bar
            phi_bar = sine * phi_bar
            now = []
            for i in range(column + 1):
                value = 1.0 / betas[i] if i == column else 0.0 * one
                if i < len(coefs_old):
                    value = value - old_eps * coefs_old[i]
                if i < len(coefs_new):
                    value = value - delta * coefs_new[i]
                now.append(value / gamma)
            coefs_old, coefs_new = coefs_new, now
            coefs_x = [
                (coefs_x[i] if i < len(coefs_x) else 0.0) + phi * now[i]
                for i in range(column + 1)
            ]

        if k == 0:
            phi_bar = beta
            betas = [beta]
        else:
            betas.append(beta)
            rotate(alpha_prev, beta, k - 1)
        scales = (1.0 / beta, None if k == 0 else beta / beta_prev, alpha / beta)
        next_res = scales[0] * q_m - scales[2] * res_m[k]
        next_lam = scales[0] * (q_m * inv_mort) - scales[2] * lam
        if k > 0:
            next_res = next_res - scales[1] * res_m[k - 1]
            next_lam = next_lam - scales[1] * mults[k - 1]
        res_m.append(next_res)
        mults.append(next_lam)
        if k + 1 < ITERS:
            lams[k + 1] = next_lam
            lam_start(k + 1)
        ry_local = out_pass(k + 1, scales) + fold(next_lam * next_res)
        beta_prev, alpha_prev = beta, alpha

    parity = ITERS % 2
    acc[parity, 0, 0:1] = ry_local
    acc[parity, 0, 1:8] = jnp.zeros((7, 128), F32)
    red_start(parity, 0)
    for number in range(last_stage):
        red_next(parity, number)
    total = red_wait(parity, last_stage)
    rotate(alpha_prev, jnp.sqrt(jnp.sum(total[0:1], axis=1, keepdims=True)), ITERS - 1)

    @pl.loop(0, slab)
    def _(l):
        value = coefs_x[0] * ys[0, l + 2]
        for k in range(1, ITERS):
            value = value + coefs_x[k] * ys[k, l + 2]
        x_ref[0, l] = value

    value = coefs_x[0] * mults[0]
    for k in range(1, ITERS):
        value = value + coefs_x[k] * mults[k]
    xm_ref[...] = value


def on_device(regions, spaces, *args):
    f_cells, g_mortar, rows = args[0], args[1], args[5].shape[1]
    slab, ny, nz = f_cells.shape[1:]
    mort = g_mortar.shape[1]
    steps = radices(spaces)
    slots = max([regions * steps[0]] + steps)
    vmem = pl.BlockSpec(memory_space=pltpu.VMEM)
    hbm = pl.BlockSpec(memory_space=pl.ANY)
    smem = pl.BlockSpec(memory_space=pltpu.SMEM)
    field = lambda *lead: pltpu.VMEM(lead + (ny, nz), F32)
    coarse = lambda *lead: pltpu.VMEM(lead + (ny // 2, nz), F32)
    dma = lambda *shape: pltpu.SemaphoreType.DMA(shape)
    return pl.pallas_call(
        functools.partial(kernel, regions, spaces),
        out_shape=(
            jax.ShapeDtypeStruct(f_cells.shape, F32),
            jax.ShapeDtypeStruct(g_mortar.shape, F32),
        ),
        in_specs=[hbm] * 4 + [smem] + [hbm] * 4 + [smem],
        out_specs=(vmem, vmem),
        scratch_shapes=[
            *(pltpu.VMEM(args[i].shape, args[i].dtype) for i in (0, 1, 2, 3, 5, 6, 7, 8)),
            dma(8),
            pltpu.VMEM((rows, 2 * mort), BF16),
            pltpu.VMEM((4 * ny, rows), BF16),
            field(slab + 4),
            field(slab + 4),
            field(slab + 2),
            field(slab + 2),
            field(slab + 4),
            field(slab + 2),
            field(slab + 2),
            field(ITERS + 1, slab + 4),
            field(3, slab),
            coarse(slab // 2 + 2),
            coarse(slab // 2 + 4),
            coarse(2),
            coarse(2),
            field(),
            pltpu.VMEM((3, 1, rows), F32),
            pltpu.VMEM((2, 3, 1, rows), F32),
            pltpu.VMEM(((slab + 2) * ny, 2 * mort), F32),
            pltpu.VMEM((3, regions, 1, mort), F32),
            pltpu.VMEM((ITERS, 1, mort), F32),
            pltpu.VMEM((1, mort), F32),
            pltpu.VMEM((1, mort), F32),
            pltpu.VMEM((2, len(steps), 8, 128), F32),
            pltpu.VMEM((2, len(steps), slots, 8, 128), F32),
            dma(5, 2),
            dma(5, 2),
            dma(3, regions),
            dma(3, regions),
            dma(2),
            dma(2, len(steps), slots),
            dma(2, len(steps), slots),
        ],
        compiler_params=pltpu.CompilerParams(
            collective_id=0, has_side_effects=True, vmem_limit_bytes=48 * 1024 * 1024
        ),
    )(*args)


def solution(mesh):
    in_specs = (
        P("region", "space", None, None),
        P("region", "space"),
        P("region", "space", None, None),
        P("region", "space", None, None),
        P(),
        P("space", None),
        P("space", None),
        P("space", None),
        P("space", None),
        P("space", None),
    )
    out_specs = (P("region", "space", None, None), P("region", "space"))
    return jax.shard_map(
        functools.partial(on_device, mesh.shape["region"], mesh.shape["space"]),
        mesh=mesh, in_specs=in_specs, out_specs=out_specs, check_vma=False,
    )
```

```python
import functools

import jax
import jax.numpy as jnp
from jax import lax
from jax.experimental import pallas as pl
from jax.experimental.pallas import tpu as pltpu
from jax.sharding import PartitionSpec as P

ZONES = 16
ITERS = 4
OMEGA = 0.8
STAB = 0.05
F32 = jnp.float32
BF16 = jnp.bfloat16
MESH = pl.DeviceIdType.MESH


def radices(count):
    found = []
    while count > 1:
        step = 4 if count % 4 == 0 else (2 if count % 2 == 0 else count)
        found.append(step)
        count //= step
    return found or [1]


def kernel(
    regions,
    spaces,
    f_hbm,
    g_hbm,
    mask_hbm,
    zone_hbm,
    zcoef_ref,
    mort_hbm,
    stokes_hbm,
    darcy_hbm,
    weight_hbm,
    tiles_ref,
    x_ref,
    xm_ref,
    f_ref,
    g_ref,
    mask_ref,
    zone_ref,
    mort_ref,
    stokes_ref,
    darcy_ref,
    weight_ref,
    in_sem,
    one_hot,
    lhs,
    ar,
    act,
    diag,
    inv,
    ay,
    q,
    ae,
    ys,
    rs,
    icoarse,
    s1,
    spack,
    srecv,
    tmp,
    meta,
    metax,
    mx,
    lamx,
    lams,
    part,
    prow,
    acc,
    red,
    halo_send,
    halo_recv,
    lam_send,
    lam_recv,
    part_sem,
    red_send,
    red_recv,
):
    copies = [
        pltpu.make_async_copy(src, dst, in_sem.at[i])
        for i, (src, dst) in enumerate((
            (mask_hbm, mask_ref),
            (zone_hbm, zone_ref),
            (f_hbm, f_ref),
            (g_hbm, g_ref),
            (mort_hbm, mort_ref),
            (stokes_hbm, stokes_ref),
            (darcy_hbm, darcy_ref),
            (weight_hbm, weight_ref),
        ))
    ]
    for copy in copies:
        copy.start()
    reg = lax.axis_index("region")
    pos = lax.axis_index("space")
    slab = f_ref.shape[1]
    ny, nz = f_ref.shape[2], f_ref.shape[3]
    nc = slab // 2
    hy = ny // 2
    mort = g_ref.shape[1]
    rows = mort_ref.shape[1]
    has_left = pos > 0
    has_right = pos < spaces - 1
    sides = ((-1, has_left), (1, has_right))
    first_region = reg == 0

    lane = lax.broadcasted_iota(jnp.int32, (ny, nz), 1)
    row = lax.broadcasted_iota(jnp.int32, (ny, nz), 0)
    layer_lane = reg * (nz - 1)
    clane = lax.broadcasted_iota(jnp.int32, (hy, nz), 1)
    crow = lax.broadcasted_iota(jnp.int32, (hy, nz), 0)
    ceven = clane % 2 == 0

    stages = []
    stride = 1
    for number, radix in enumerate(radices(spaces)):
        digit = (pos // stride) % radix
        base = pos - digit * stride
        peers = []
        for d_reg in range(regions if number == 0 else 1):
            for j in range(radix):
                if d_reg == 0 and j == 0:
                    continue
                peers.append((
                    d_reg * radix + j,
                    ((reg + d_reg) % regions, base + ((digit + j) % radix) * stride),
                ))
        stages.append(peers)
        stride *= radix

    barrier = pltpu.get_barrier_semaphore()
    waits = 0
    for peers in stages:
        for _, who in peers:
            pl.semaphore_signal(barrier, inc=1, device_id=who, device_id_type=MESH)
            waits += 1
    for step, there in sides:
        for d_reg in range(regions):
            @pl.when(there)
            def _():
                pl.semaphore_signal(
                    barrier, inc=1, device_id=((reg + d_reg) % regions, pos + step),
                    device_id_type=MESH,
                )
    beside = has_left.astype(jnp.int32) + has_right.astype(jnp.int32)
    pl.semaphore_wait(barrier, waits + regions * beside)

    def halo(kind, step, src, dst):
        side = (step + 1) // 2
        return pltpu.make_async_remote_copy(
            src_ref=src, dst_ref=dst,
            send_sem=halo_send.at[kind, side], recv_sem=halo_recv.at[kind, 1 - side],
            device_id=(reg, pos + step), device_id_type=MESH,
        )

    def start_halo(kind, src_of, dst_of):
        for step, there in sides:
            @pl.when(there)
            def _():
                halo(kind, step, src_of(step), dst_of(step)).start()

    def wait_halo(kind, src_of, dst_of):
        for step, there in sides:
            @pl.when(there)
            def _():
                halo(kind, step, src_of(step), dst_of(step)).wait_send()
                pltpu.make_async_remote_copy(
                    src_ref=src_of(-step), dst_ref=dst_of(-step),
                    send_sem=halo_send.at[kind, (1 - step) // 2],
                    recv_sem=halo_recv.at[kind, (step + 1) // 2],
                    device_id=(reg, pos + step), device_id_type=MESH,
                ).wait_recv()

    zero = jnp.zeros((ny, nz), F32)

    def clear(side_lo, there):
        @pl.when(jnp.logical_not(there))
        def _():
            for d in range(2):
                at = side_lo * (slab + 2) + d
                ar[at] = zero
                for k in range(ITERS):
                    ys[k, at] = zero
                srecv[side_lo] = jnp.zeros((hy, nz), F32)
            q[side_lo * (slab + 1)] = zero
            for k in range(3):
                metax[side_lo, k] = jnp.zeros((1, rows), F32)
            for d_reg in range(regions):
                lamx[2 * side_lo, d_reg] = jnp.zeros((1, mort), F32)

    f_src = lambda step: f_ref.at[0, pl.ds(0 if step < 0 else slab - 1, 1)]
    f_dst = lambda step: q.at[pl.ds(slab + 1 if step < 0 else 0, 1)]
    ar_src = lambda step: ar.at[pl.ds(2 if step < 0 else slab, 2)]
    ar_dst = lambda step: ar.at[pl.ds(slab + 2 if step < 0 else 0, 2)]
    meta_src = lambda step: meta
    meta_dst = lambda step: metax.at[1 if step < 0 else 0]

    def y_src(k):
        return lambda step: ys.at[k, pl.ds(2 if step < 0 else slab, 2)]

    def y_dst(k):
        return lambda step: ys.at[k, pl.ds(slab + 2 if step < 0 else 0, 2)]

    s_src = lambda step: spack.at[0 if step < 0 else 1]
    s_dst = lambda step: srecv.at[1 if step < 0 else 0]

    def react_layer(l):
        ids = zone_ref[0, l]
        value = jnp.zeros((ny, nz), F32)
        for zone in range(ZONES):
            value = jnp.where(ids == zone, zcoef_ref[zone], value)
        ar[l + 2] = jnp.where(mask_ref[0, l] != 0, value, 0.0)

    for copy in copies:
        copy.wait()

    @pl.loop(0, slab)
    def _(l):
        react_layer(l)

    start_halo(1, ar_src, ar_dst)
    clear(0, has_left)
    clear(1, has_right)

    lane_row = lax.broadcasted_iota(jnp.int32, (1, rows), 1)
    limit = jnp.zeros((1, rows), jnp.int32)
    for tile in range(rows // 128):
        limit = jnp.where(lane_row // 128 == tile, tiles_ref[0, tile], limit)
    coef = jnp.where(lane_row % 128 < limit, weight_ref[...], 0.0)
    side_sign = jnp.where(first_region, 1.0, -1.0).astype(F32)
    meta[0] = mort_ref[...].astype(F32)
    meta[1] = jnp.where(first_region, stokes_ref[...], darcy_ref[...]).astype(F32)
    meta[2] = coef * side_sign
    start_halo(2, meta_src, meta_dst)
    start_halo(0, f_src, f_dst)

    @pl.loop(0, slab)
    def _(l):
        q[l + 1] = f_ref[0, l]
        rs[0, l] = f_ref[0, l]

    def split(value):
        high = value.astype(BF16).astype(F32)
        rest = value - high
        mid = rest.astype(BF16).astype(F32)
        return high, mid, rest - mid

    face = lax.broadcasted_iota(jnp.int32, (ny, rows), 0).astype(F32)
    multiplier = lax.broadcasted_iota(jnp.int32, (128, 2 * mort), 1).astype(F32)

    def set_one_hot(source):
        tiles = rows // 128
        listed = [source[0, :, pl.ds(128 * t, 128)] for t in range(tiles)]
        listed.append(jnp.zeros((128 - tiles, 128), F32))
        down = jnp.transpose(jnp.concatenate(listed, axis=0))
        for t in range(tiles):
            hit = multiplier == down[:, t : t + 1]
            one_hot[pl.ds(128 * t, 128), :] = jnp.where(hit, 1.0, 0.0).astype(BF16)

    def set_layers(source, first_layer, layers, target):
        face_row, coef_row = source[1], source[2]
        high, mid, _ = split(coef_row)
        for i in range(layers):
            start = jnp.asarray((first_layer + i) * ny, jnp.int32).astype(F32)
            hit = face == face_row - start
            lhs[pl.ds(2 * i * ny, ny), :] = jnp.where(hit, high, 0.0).astype(BF16)
            lhs[pl.ds((2 * i + 1) * ny, ny), :] = jnp.where(hit, mid, 0.0).astype(BF16)
        value = jnp.dot(
            lhs[pl.ds(0, 2 * layers * ny), :], one_hot[...], preferred_element_type=F32
        )
        for i in range(layers):
            at = (target + i) * ny
            at = pl.ds(at if isinstance(at, int) else pl.multiple_of(at, ny), ny)
            mx[at, :] = value[2 * i * ny : (2 * i + 1) * ny] + value[
                (2 * i + 1) * ny : (2 * i + 2) * ny
            ]

    set_one_hot(meta)

    @pl.loop(0, slab // 2)
    def _(pair):
        set_layers(meta, 2 * pair, 2, 1 + 2 * pair)

    high, mid, low = split(meta[2] * meta[2])
    piece = lax.broadcasted_iota(jnp.int32, (16, rows), 0)
    pieces = jnp.where(
        piece == 0, high, jnp.where(piece == 1, mid, jnp.where(piece == 2, low, 0.0))
    )
    squares = jnp.sum(
        jnp.dot(pieces.astype(BF16), one_hot[...], preferred_element_type=F32),
        axis=0, keepdims=True,
    )
    own_half = lambda v: jnp.where(first_region, v[:, :mort], v[:, mort:])
    other_half = lambda v: jnp.where(first_region, v[:, mort:], v[:, :mort])
    inv_mort = 1.0 / (STAB + own_half(squares) / 3.0)

    wait_halo(2, meta_src, meta_dst)
    set_one_hot(metax.at[0])
    set_layers(metax.at[0], slab - 1, 1, 0)
    set_one_hot(metax.at[1])
    set_layers(metax.at[1], 0, 1, slab + 1)
    wait_halo(1, ar_src, ar_dst)

    @pl.loop(0, slab + 4)
    def _(l):
        act[l] = jnp.where(ar[l] > 0.0, 1.0, 0.0)

    @pl.loop(0, slab + 2)
    def _(l):
        value = jnp.where(ar[l + 1] > 0.0, 6.0 + ar[l + 1], 1.0)
        diag[l] = value
        inv[l] = OMEGA / value

    def pair_sum(total):
        tmp[...] = total
        v = tmp[pl.ds(0, hy, stride=2), :] + tmp[pl.ds(1, hy, stride=2), :]
        return v + jnp.where(ceven, pltpu.roll(v, nz - 1, 1), pltpu.roll(v, 1, 1))

    @pl.loop(0, nc + 2)
    def _(b):
        icoarse[b] = OMEGA / (12.0 + 0.25 * pair_sum(ar[2 * b] + ar[2 * b + 1]))

    def in_layer(c):
        total = jnp.where(row == 0, 0.0, pltpu.roll(c, 1, 0))
        total = total + jnp.where(row == ny - 1, 0.0, pltpu.roll(c, ny - 1, 0))
        total = total + jnp.where(lane == 0, 0.0, pltpu.roll(c, 1, 1))
        return total + jnp.where(lane == nz - 1, 0.0, pltpu.roll(c, nz - 1, 1))

    def neighbours(ref, at):
        return in_layer(ref[at]) + (ref[at - 1] + ref[at + 1])

    def coarse_in_layer(c):
        total = jnp.where(crow == 0, 0.0, pltpu.roll(c, 1, 0))
        total = total + jnp.where(crow == hy - 1, 0.0, pltpu.roll(c, hy - 1, 0))
        total = total + jnp.where(clane < 2, 0.0, pltpu.roll(c, 2, 1))
        return total + jnp.where(clane >= nz - 2, 0.0, pltpu.roll(c, nz - 2, 1))

    def scale_first(l):
        ae[l] = act[l + 1] * (inv[l] * q[l])

    def coarse_first(b):
        total = jnp.zeros((ny, nz), F32)
        for d in range(2):
            l = 2 * b + d + 1
            total = total + (0.2 * q[l] + act[l + 1] * neighbours(ae, l))
        s1[b + 2] = icoarse[b + 1] * pair_sum(total)

    def send_coarse():
        spack[0] = jnp.where(ceven, s1[2], s1[3])
        spack[1] = jnp.where(ceven, s1[nc], s1[nc + 1])
        start_halo(3, s_src, s_dst)

    def receive_coarse():
        wait_halo(3, s_src, s_dst)
        for side, at in ((0, 0), (1, nc + 2)):
            v = srecv[side]
            s1[at] = jnp.where(ceven, v, pltpu.roll(v, 1, 1))
            s1[at + 1] = jnp.where(ceven, pltpu.roll(v, nz - 1, 1), v)

    def second_block(b):
        s2 = 1.2 * s1[b + 1] + 2.0 * icoarse[b] * (
            coarse_in_layer(s1[b + 1]) + (s1[b] + s1[b + 2])
        )
        tmp[pl.ds(0, hy, stride=2), :] = s2
        tmp[pl.ds(1, hy, stride=2), :] = s2
        return tmp[...]

    e2 = ay

    def second_all():
        up = second_block(0)
        e2[0] = inv[0] * q[0] + up
        ae[0] = act[1] * e2[0]
        up = second_block(nc + 1)
        e2[slab + 1] = inv[slab + 1] * q[slab + 1] + up
        ae[slab + 1] = act[slab + 2] * e2[slab + 1]

        @pl.loop(1, nc + 1)
        def _(b):
            up = second_block(b)
            for d in range(2):
                l = 2 * b - 1 + d
                value = inv[l] * q[l] + up
                e2[l] = value
                ae[l] = act[l + 1] * value

    def last_layer(l):
        return 0.2 * e2[l] + inv[l] * (q[l] + act[l + 1] * neighbours(ae, l))

    def finish_image():
        @pl.loop(1, slab + 1)
        def _(l):
            e2[l] = last_layer(l)

    def fold(v):
        out = v[:, 0:128]
        for k in range(1, v.shape[1] // 128):
            out = out + v[:, 128 * k : 128 * (k + 1)]
        return out

    def lay_sum(v):
        return jnp.sum(v.reshape(ny // 8, 8, nz), axis=0)

    def red_copy(parity, number, slot, who):
        return pltpu.make_async_remote_copy(
            src_ref=acc.at[parity, number], dst_ref=red.at[parity, number, slot],
            send_sem=red_send.at[parity, number, slot],
            recv_sem=red_recv.at[parity, number, slot],
            device_id=who, device_id_type=MESH,
        )

    def red_start(parity, number):
        for slot, who in stages[number]:
            red_copy(parity, number, slot, who).start()

    def red_wait(parity, number):
        for slot, who in stages[number]:
            red_copy(parity, number, slot, who).wait()
        total = acc[parity, number]
        for slot, _ in stages[number]:
            total = total + red[parity, number, slot]
        return total

    def red_next(parity, number):
        acc[parity, number + 1] = red_wait(parity, number)
        red_start(parity, number + 1)

    last_stage = len(stages) - 1

    def lam_copy(k, step, d_reg, sending):
        there = step if sending else -step
        return pltpu.make_async_remote_copy(
            src_ref=lams.at[k], dst_ref=lamx.at[1 - there, d_reg],
            send_sem=lam_send.at[there + 1, d_reg], recv_sem=lam_recv.at[1 - there, d_reg],
            device_id=((reg + d_reg) % regions, pos + step), device_id_type=MESH,
        )

    def lam_each(action):
        for step, there in ((-1, has_left), (0, None), (1, has_right)):
            for d_reg in range(regions):
                if step == 0:
                    if d_reg:
                        action(step, d_reg)
                else:
                    pl.when(there)(functools.partial(action, step, d_reg))

    def lam_start(k):
        lam_each(lambda step, d_reg: lam_copy(k, step, d_reg, True).start())

    def lam_wait(k):
        def both(step, d_reg):
            lam_copy(k, step, d_reg, True).wait_send()
            lam_copy(k, step, d_reg, False).wait_recv()

        lam_each(both)

    def paired(offset, own):
        mine, others = own, lamx[offset, 1]
        return jnp.concatenate(
            [jnp.where(first_region, mine, others), jnp.where(first_region, others, mine)], axis=1
        )

    def apply_cells(k, l):
        y = ys[k, l + 1]
        q[l] = diag[l] * y - act[l + 1] * neighbours(ay, l + 1)

    def add_face(l, lam_row):
        at = pl.ds(l * ny if isinstance(l, int) else pl.multiple_of(l * ny, ny), ny)
        col = jnp.sum(mx[at, :] * lam_row, axis=1, keepdims=True)
        q[l] = q[l] + jnp.where(lane == layer_lane, col, 0.0)

    wait_halo(0, f_src, f_dst)

    @pl.loop(0, slab + 2)
    def _(l):
        scale_first(l)

    @pl.loop(0, nc)
    def _(b):
        coarse_first(b)

    send_coarse()
    res_m = [g_ref[...]]
    lam = g_ref[...] * inv_mort
    lams[0] = lam
    lam_start(0)
    receive_coarse()
    second_all()
    finish_image()

    one = jnp.ones((1, 1), F32)
    mults = [lam]
    beta_prev = None
    ry_local = None
    coefs_old, coefs_new, coefs_x = [], [], []
    cosine, sine = -one, 0.0 * one
    delta_bar, epsilon = 0.0 * one, 0.0 * one
    phi_bar = None

    def out_pass(k, scales):
        def body(l, total):
            value = e2[l + 1]
            if scales is None:
                resid = rs[0, l]
            else:
                s_q, s_old, s_now = scales
                value = s_q * value - s_now * ys[k - 1, l + 2]
                resid = s_q * q[l + 1] - s_now * rs[(k - 1) % 3, l]
                if s_old is not None:
                    value = value - s_old * ys[k - 2, l + 2]
                    resid = resid - s_old * rs[(k - 2) % 3, l]
                rs[k % 3, l] = resid
            ys[k, l + 2] = value
            return total + lay_sum(value * resid)

        total = jnp.zeros((8, nz), F32)
        total = lax.fori_loop(0, 2, body, total)
        total = lax.fori_loop(slab - 2, slab, body, total)
        if k < ITERS:
            start_halo(4, y_src(k), y_dst(k))
        total = lax.fori_loop(2, slab - 2, body, total)
        return jnp.sum(total, axis=0, keepdims=True)

    ry_local = out_pass(0, None) + fold(lam * res_m[0])
    for k in range(ITERS):
        parity = k % 2
        lam = mults[k]

        @pl.loop(2, slab + 2)
        def _(l):
            ay[l] = act[l] * ys[k, l]

        @pl.loop(2, slab)
        def _(l):
            apply_cells(k, l)

        lam_wait(k)
        own_pair = paired(1, lam)

        def operate(l, carry):
            add_face(l, own_pair)
            y = ys[k, l + 1]
            u = jnp.where(first_region, y[:, 0:1], y[:, nz - 1 : nz])
            at = pl.ds(pl.multiple_of(l * ny, ny), ny)
            prod, old, prt = carry
            prod = prod + lay_sum(y * q[l])
            if k > 0:
                old = old + lay_sum(y * rs[(k - 1) % 3, l - 1])
            prt = prt + jnp.sum((mx[at, :] * u).reshape(ny // 8, 8, 2 * mort), axis=0)
            scale_first(l)
            return prod, old, prt

        carry = (
            jnp.zeros((8, nz), F32),
            jnp.zeros((8, nz), F32),
            jnp.zeros((8, 2 * mort), F32),
        )
        carry = lax.fori_loop(2, slab, operate, carry)

        @pl.loop(1, nc - 1)
        def _(b):
            coarse_first(b)

        wait_halo(4, y_src(k), y_dst(k))
        for l in (0, 1, slab + 2, slab + 3):
            ay[l] = act[l] * ys[k, l]
        apply_cells(k, 1)
        apply_cells(k, slab)
        carry = operate(jnp.int32(1), carry)
        prod, old, prt = operate(jnp.int32(slab), carry)
        apply_cells(k, 0)
        apply_cells(k, slab + 1)
        add_face(0, paired(0, lamx[0, 0]))
        add_face(slab + 1, paired(2, lamx[2, 0]))
        scale_first(0)
        scale_first(slab + 1)
        coarse_first(0)
        coarse_first(nc - 1)
        send_coarse()
        partial_rows = jnp.sum(prt, axis=0, keepdims=True)
        prow[...] = other_half(partial_rows)
        part_copy = pltpu.make_async_remote_copy(
            src_ref=prow, dst_ref=part, send_sem=part_sem.at[0], recv_sem=part_sem.at[1],
            device_id=((reg + 1) % regions, pos), device_id_type=MESH,
        )
        part_copy.start()
        prod_row = jnp.sum(prod, axis=0, keepdims=True)
        prod_row = prod_row + fold(own_pair * partial_rows) - STAB * fold(lam * lam)
        old_row = jnp.sum(old, axis=0, keepdims=True)
        if k > 0:
            old_row = old_row + fold(lam * res_m[k - 1])
        acc[parity, 0, 0:1] = ry_local
        acc[parity, 0, 1:2] = prod_row
        acc[parity, 0, 2:3] = old_row
        acc[parity, 0, 3:8] = jnp.zeros((5, 128), F32)
        red_start(parity, 0)
        for number in range(last_stage):
            red_next(parity, number)
        receive_coarse()
        part_copy.wait()
        q_m = own_half(partial_rows) + part[...] - STAB * lam
        second_all()
        finish_image()
        total = red_wait(parity, last_stage)
        sums = jnp.sum(total, axis=1, keepdims=True)
        ry, yky, yr = sums[0:1], sums[1:2], sums[2:3]
        beta = jnp.sqrt(ry)
        alpha = yky / ry
        if k > 0:
            alpha = alpha - yr / beta_prev
        def rotate(alpha_now, beta_next, column):
            nonlocal cosine, sine, delta_bar, epsilon, phi_bar
            nonlocal coefs_old, coefs_new, coefs_x
            old_eps = epsilon
            delta = cosine * delta_bar + sine * alpha_now
            gamma_bar = sine * delta_bar - cosine * alpha_now
            epsilon = sine * beta_next
            delta_bar = -cosine * beta_next
            gamma = jnp.sqrt(gamma_bar * gamma_bar + beta_next * beta_next)
            cosine = gamma_bar / gamma
            sine = beta_next / gamma
            phi = cosine * phi_bar
            phi_bar = sine * phi_bar
            now = []
            for i in range(column + 1):
                value = 1.0 / betas[i] if i == column else 0.0 * one
                if i < len(coefs_old):
                    value = value - old_eps * coefs_old[i]
                if i < len(coefs_new):
                    value = value - delta * coefs_new[i]
                now.append(value / gamma)
            coefs_old, coefs_new = coefs_new, now
            coefs_x = [
                (coefs_x[i] if i < len(coefs_x) else 0.0) + phi * now[i]
                for i in range(column + 1)
            ]

        if k == 0:
            phi_bar = beta
            betas = [beta]
        else:
            betas.append(beta)
            rotate(alpha_prev, beta, k - 1)
        scales = (1.0 / beta, None if k == 0 else beta / beta_prev, alpha / beta)
        next_res = scales[0] * q_m - scales[2] * res_m[k]
        next_lam = scales[0] * (q_m * inv_mort) - scales[2] * lam
        if k > 0:
            next_res = next_res - scales[1] * res_m[k - 1]
            next_lam = next_lam - scales[1] * mults[k - 1]
        res_m.append(next_res)
        mults.append(next_lam)
        if k + 1 < ITERS:
            lams[k + 1] = next_lam
            lam_start(k + 1)
        ry_local = out_pass(k + 1, scales) + fold(next_lam * next_res)
        beta_prev, alpha_prev = beta, alpha

    parity = ITERS % 2
    acc[parity, 0, 0:1] = ry_local
    acc[parity, 0, 1:8] = jnp.zeros((7, 128), F32)
    red_start(parity, 0)
    for number in range(last_stage):
        red_next(parity, number)
    total = red_wait(parity, last_stage)
    rotate(alpha_prev, jnp.sqrt(jnp.sum(total[0:1], axis=1, keepdims=True)), ITERS - 1)

    @pl.loop(0, slab)
    def _(l):
        value = coefs_x[0] * ys[0, l + 2]
        for k in range(1, ITERS):
            value = value + coefs_x[k] * ys[k, l + 2]
        x_ref[0, l] = value

    value = coefs_x[0] * mults[0]
    for k in range(1, ITERS):
        value = value + coefs_x[k] * mults[k]
    xm_ref[...] = value


def on_device(regions, spaces, *args):
    f_cells, g_mortar, rows = args[0], args[1], args[5].shape[1]
    slab, ny, nz = f_cells.shape[1:]
    mort = g_mortar.shape[1]
    steps = radices(spaces)
    slots = max([regions * steps[0]] + steps)
    vmem = pl.BlockSpec(memory_space=pltpu.VMEM)
    hbm = pl.BlockSpec(memory_space=pltpu.HBM)
    smem = pl.BlockSpec(memory_space=pltpu.SMEM)
    field = lambda *lead: pltpu.VMEM(lead + (ny, nz), F32)
    coarse = lambda *lead: pltpu.VMEM(lead + (ny // 2, nz), F32)
    dma = lambda *shape: pltpu.SemaphoreType.DMA(shape)
    return pl.pallas_call(
        functools.partial(kernel, regions, spaces),
        out_shape=(
            jax.ShapeDtypeStruct(f_cells.shape, F32),
            jax.ShapeDtypeStruct(g_mortar.shape, F32),
        ),
        in_specs=[hbm] * 4 + [smem] + [hbm] * 4 + [smem],
        out_specs=(vmem, vmem),
        scratch_shapes=[
            *(pltpu.VMEM(args[i].shape, args[i].dtype) for i in (0, 1, 2, 3, 5, 6, 7, 8)),
            dma(8),
            pltpu.VMEM((rows, 2 * mort), BF16),
            pltpu.VMEM((4 * ny, rows), BF16),
            field(slab + 4),
            field(slab + 4),
            field(slab + 2),
            field(slab + 2),
            field(slab + 4),
            field(slab + 2),
            field(slab + 2),
            field(ITERS + 1, slab + 4),
            field(3, slab),
            coarse(slab // 2 + 2),
            coarse(slab // 2 + 4),
            coarse(2),
            coarse(2),
            field(),
            pltpu.VMEM((3, 1, rows), F32),
            pltpu.VMEM((2, 3, 1, rows), F32),
            pltpu.VMEM(((slab + 2) * ny, 2 * mort), F32),
            pltpu.VMEM((3, regions, 1, mort), F32),
            pltpu.VMEM((ITERS, 1, mort), F32),
            pltpu.VMEM((1, mort), F32),
            pltpu.VMEM((1, mort), F32),
            pltpu.VMEM((2, len(steps), 8, 128), F32),
            pltpu.VMEM((2, len(steps), slots, 8, 128), F32),
            dma(5, 2),
            dma(5, 2),
            dma(3, regions),
            dma(3, regions),
            dma(2),
            dma(2, len(steps), slots),
            dma(2, len(steps), slots),
        ],
        compiler_params=pltpu.CompilerParams(
            collective_id=0, has_side_effects=True, vmem_limit_bytes=56 * 1024 * 1024
        ),
    )(*args)


def solution(mesh):
    in_specs = (
        P("region", "space", None, None),
        P("region", "space"),
        P("region", "space", None, None),
        P("region", "space", None, None),
        P(),
        P("space", None),
        P("space", None),
        P("space", None),
        P("space", None),
        P("space", None),
    )
    out_specs = (P("region", "space", None, None), P("region", "space"))
    return jax.shard_map(
        functools.partial(on_device, mesh.shape["region"], mesh.shape["space"]),
        mesh=mesh, in_specs=in_specs, out_specs=out_specs, check_vma=False,
    )
```
